512 devices in a mesh: ctx: 64 (over x, y_lo, z), cand: 8 (over y_hi, core).
Axes of the slice: x: 4, y: 8 (y_hi: 4, y_lo: 2; y = y_hi * 2 + y_lo), z: 8, core: 2. Of those that a mesh axis runs over, the one named last changes fastest.
Arguments:
- history: bfloat16 [8192, 1024], P('ctx', 'cand'), may hold values from -6 to 6
- head_weights: bfloat16 [1024, 4096], P(None, 'cand'), may hold values from -0.1875 to 0.1875
- merge_weights: bfloat16 [1024, 1024], P('cand'), may hold values from -0.1875 to 0.1875
- cand_table: bfloat16 [4096, 1024], P('cand'), may hold values from -6 to 6
- user_weights: bfloat16 [1024, 512], P('cand'), may hold values from -0.1875 to 0.1875
- item_weights: bfloat16 [1024, 512], replicated, may hold values from -0.1875 to 0.1875
- score_weights: float32 [512], replicated, may hold values from -0.4 to 0.4
- request_points: int32 [256], replicated, may hold values from 0 to 8191, as said below
- candidate_owner: int32 [256, 512], P('ctx'), may hold values from 0 to 7
- candidate_row: int32 [256, 512], P('ctx'), may hold values from 0 to 511
- relevance: int32 [256, 512], P('ctx'), may hold values from 0 to 3
Outputs:
- losses: float32 [256], P('ctx')
- history_grad: float32 [8192, 1024], P('ctx', 'cand')
- grad_heads: float32 [1024, 4096], P('ctx', 'cand')
- grad_merge: float32 [1024, 1024], P('cand', 'ctx')
The draws below stay inside these ranges and needn't reach their ends.
Inputs may be any that keep to these rules, and one draw needn't show every extreme that they name: `request_points`: the last request is made at the last position of the history.
All inputs are finite; a program needn't handle non-finite values.
Results may differ from the reference program's by a relative error of at most 0.012.
The reference program's roundings to bfloat16 on the way (of `x_low`, `project`, `weight`, `gated`, `layer_out`, `d_attended`, `d_logit` and `d_before`) count: a program that leaves them out, or rounds other values in their place, can miss the bound.
Values may be sent and summed in bfloat16 or wider, within the bound.
No kernel may reach another device: no remote copies, remote signals or barrier semaphores. Data moves between devices by JAX's collectives and lax.ppermute only.
A program may use at most 64 MiB of HBM per device.

```python
import math
import jax
import jax.numpy as jnp
from jax import lax

D = 1024
HEADS = 8
HEAD = 128
NCAND = 512
HIDDEN_SIZE = 512
ROWS_DEV = 512
SEQ = 8192
REQUESTS = 256
ROWS = 4096
N_CAND = 8


def draw_request_points(key, part):
    key = jax.random.fold_in(key, 7)
    points = jax.random.randint(key, (REQUESTS,), 0, SEQ, dtype=jnp.int32)
    return points.at[REQUESTS - 1].set(SEQ - 1)


def set_ends(entries, stream_key, smallest, top_value):
    shape = entries.shape
    spot = [jax.random.randint(jax.random.fold_in(stream_key, axis), (), 0, shape[axis]) for axis in range(len(shape))]
    entries = entries.at[tuple(spot)].set(smallest)
    longest = shape.index(max(shape))
    spot[longest] = (spot[longest] + 1) % shape[longest]
    return entries.at[tuple(spot)].set(top_value)


def block_levels(rng, extent, split, smallest, largest):
    def one(dim, shards_of):
        draws = jax.random.uniform(jax.random.fold_in(jax.random.fold_in(rng, 6), dim), (shards_of,), jnp.float32, smallest / len(split), largest / len(split))
        return jnp.repeat(jnp.exp(draws), extent[dim] // shards_of).reshape((-1,) + (1,) * (len(extent) - dim - 1))

    loudness = one(*split[0])
    for cut in split[1:]:
        loudness = loudness * one(*cut)
    return loudness


def scatter_about(own_key, shape, scale, reach, cuts=(), held_as=jnp.bfloat16):
    factor_of = block_levels(own_key, shape, cuts, -0.22, 0.18) if cuts else 1.0
    array = jax.random.normal(own_key, shape, jnp.float32) * scale * factor_of
    return jnp.minimum(jnp.maximum(array, -reach), reach).astype(held_as)


def setup_inputs(seed: int = 0) -> dict:
    key_list = jax.random.split(jax.random.key(seed), 12)
    history = scatter_about(key_list[0], (SEQ, D), 1.0, 6.0, ((0, 64), (1, 8)))
    head_weights = scatter_about(key_list[1], (D, 4 * HEADS * HEAD), D ** -0.5, 0.1875, ((1, 8),))
    merge_weights = scatter_about(key_list[2], (HEADS * HEAD, D), (HEADS * HEAD) ** -0.5, 0.1875, ((0, 8),))
    cand_table = scatter_about(key_list[3], (ROWS, D), 1.0, 6.0, ((0, 8),))
    user_weights = scatter_about(key_list[4], (D, HIDDEN_SIZE), D ** -0.5, 0.1875, ((0, 8),))
    item_weights = scatter_about(key_list[5], (D, HIDDEN_SIZE), D ** -0.5, 0.1875)
    score_weights = scatter_about(key_list[6], (HIDDEN_SIZE,), 0.1, 0.4, (), jnp.float32)
    request_points = draw_request_points(jax.random.fold_in(key_list[11], 71), 0)
    candidate_owner = set_ends(jax.random.randint(key_list[8], (REQUESTS, NCAND), 0, N_CAND), jax.random.fold_in(key_list[8], 1), 0, N_CAND - 1).astype(jnp.int32)
    candidate_row = set_ends(jax.random.randint(key_list[9], (REQUESTS, NCAND), 0, ROWS_DEV), jax.random.fold_in(key_list[9], 1), 0, ROWS_DEV - 1).astype(jnp.int32)
    relevance = set_ends(jax.random.randint(key_list[10], (REQUESTS, NCAND), 0, 4), jax.random.fold_in(key_list[10], 1), 0, 3).astype(jnp.int32)
    return dict(history=history, head_weights=head_weights, merge_weights=merge_weights, cand_table=cand_table, user_weights=user_weights, item_weights=item_weights, score_weights=score_weights, request_points=request_points, candidate_owner=candidate_owner, candidate_row=candidate_row, relevance=relevance)


norm_eps = 1e-05

def silu_slope(argument):
    sigmoid_part = jax.nn.sigmoid(argument)
    return sigmoid_part * (1.0 + argument * (1.0 - sigmoid_part))

def layer_norm(argument):
    centred = argument - lax.optimization_barrier(jnp.mean(argument, -1, keepdims=True))
    inverse = lax.rsqrt(lax.optimization_barrier(jnp.mean(centred * centred, -1, keepdims=True)) + norm_eps)
    return (centred * inverse, inverse)

def norm_back(gradient, normed, inverse):
    return inverse * (gradient - lax.optimization_barrier(jnp.mean(gradient, -1, keepdims=True)) - normed * lax.optimization_barrier(jnp.mean(gradient * normed, -1, keepdims=True)))

def score_tile(queries, key_heads, query_start, key_start):
    scaling = queries.shape[-1] ** (-0.5)
    logits = jnp.dot(queries, key_heads.T, preferred_element_type=jnp.float32) * scaling
    query_place = query_start + jnp.arange(queries.shape[0], dtype=jnp.int32)
    key_place = key_start + jnp.arange(key_heads.shape[0], dtype=jnp.int32)
    allowed = key_place[None, :] <= query_place[:, None]
    divisor = (query_place + 1).astype(jnp.float32)[:, None]
    return (logits, allowed, divisor)

def head_forward(queries, key_heads, values):
    length = queries.shape[0]
    block_rows = math.gcd(512, length)
    starts = jnp.arange(0, length, block_rows, dtype=jnp.int32)

    def query_block(begin):
        block = lax.dynamic_slice_in_dim(queries, begin, block_rows, 0)
        logits, allowed, divisor = score_tile(block, key_heads, begin, 0)
        weight = jnp.where(allowed, jax.nn.silu(logits) / divisor, 0.0).astype(jnp.bfloat16)
        return jnp.dot(weight, values, preferred_element_type=jnp.float32)
    return lax.map(query_block, starts).reshape(length, queries.shape[1])

def head_backward(queries, key_heads, values, out_grads):
    length = queries.shape[0]
    block_rows = math.gcd(512, length)
    starts = jnp.arange(0, length, block_rows, dtype=jnp.int32)
    scaling = queries.shape[-1] ** (-0.5)

    def query_block(begin):
        block = lax.dynamic_slice_in_dim(queries, begin, block_rows, 0)
        grads_block = lax.dynamic_slice_in_dim(out_grads, begin, block_rows, 0)
        logits, allowed, divisor = score_tile(block, key_heads, begin, 0)
        slopes = jnp.dot(grads_block, values.T, preferred_element_type=jnp.float32)
        d_logit = jnp.where(allowed, slopes * silu_slope(logits) / divisor, 0.0).astype(jnp.bfloat16)
        return jnp.dot(d_logit, key_heads, preferred_element_type=jnp.float32) * scaling

    def key_block(begin):
        key_part = lax.dynamic_slice_in_dim(key_heads, begin, block_rows, 0)
        value_part = lax.dynamic_slice_in_dim(values, begin, block_rows, 0)
        logits, allowed, divisor = score_tile(queries, key_part, 0, begin)
        weight = jnp.where(allowed, jax.nn.silu(logits) / divisor, 0.0).astype(jnp.bfloat16)
        d_value = jnp.dot(weight.T, out_grads, preferred_element_type=jnp.float32)
        slopes = jnp.dot(out_grads, value_part.T, preferred_element_type=jnp.float32)
        d_logit = jnp.where(allowed, slopes * silu_slope(logits) / divisor, 0.0).astype(jnp.bfloat16)
        d_key = jnp.dot(d_logit.T, queries, preferred_element_type=jnp.float32) * scaling
        return (d_key, d_value)
    width = queries.shape[1]
    d_query = lax.map(query_block, starts).reshape(length, width)
    d_key, d_value = lax.map(key_block, starts)
    return (d_query, d_key.reshape(length, width), d_value.reshape(length, width))

def reference(history, head_weights, merge_weights, cand_table, user_weights, item_weights, score_weights, request_points, candidate_owner, candidate_row, relevance):
    length = history.shape[0]
    x_wide = history.astype(jnp.float32)
    x_normed, x_inverse = layer_norm(x_wide)
    x_low = x_normed.astype(jnp.bfloat16)
    before = jnp.dot(x_low, head_weights, preferred_element_type=jnp.float32)
    project = jax.nn.silu(before).astype(jnp.bfloat16)
    sections = project.reshape(length, HEADS, 4, HEAD).transpose(2, 1, 0, 3)
    gate_part, values, queries, key_heads = (sections[0], sections[1], sections[2], sections[3])
    attended = lax.map(lambda stacked: head_forward(stacked[0], stacked[1], stacked[2]), (queries, key_heads, values))
    normed, inverse = layer_norm(attended)
    gated = (normed * gate_part.astype(jnp.float32)).astype(jnp.bfloat16)
    gated_rows = gated.transpose(1, 0, 2).reshape(length, HEADS * HEAD)
    layer_out = (x_wide + jnp.dot(gated_rows, merge_weights, preferred_element_type=jnp.float32)).astype(jnp.bfloat16)
    picked = layer_out[request_points]
    user_proj = jnp.dot(picked, user_weights, preferred_element_type=jnp.float32)
    item_proj = jnp.dot(cand_table, item_weights, preferred_element_type=jnp.float32)
    row_index = (candidate_owner * ROWS_DEV + candidate_row).astype(jnp.int32)

    def request_scores(request):
        user_row, index_row, grade_row = request
        pre_score = user_row[None, :] + item_proj[index_row]
        scores = lax.optimization_barrier(jnp.sum(jax.nn.silu(pre_score) * score_weights[None, :], -1))
        log_total = jnp.log(jnp.sum(jnp.exp(scores)))
        target = (grade_row + 1).astype(jnp.float32)
        target = target / jnp.sum(target)
        request_loss = log_total - jnp.sum(target * scores)
        d_score = jnp.exp(scores - log_total) - target
        d_user = lax.optimization_barrier(jnp.sum(d_score[:, None] * score_weights[None, :] * silu_slope(pre_score), 0))
        return (request_loss, d_user)
    losses, d_user = lax.map(request_scores, (user_proj, row_index, relevance))
    d_picked = jnp.dot(d_user, user_weights.astype(jnp.float32).T, precision=lax.Precision.HIGHEST)
    d_layer = jnp.zeros((length, history.shape[1]), jnp.float32).at[request_points].add(d_picked)
    d_gated = jnp.dot(d_layer, merge_weights.astype(jnp.float32).T, precision=lax.Precision.HIGHEST)
    grad_merge = jnp.dot(gated_rows.astype(jnp.float32).T, d_layer, precision=lax.Precision.HIGHEST)
    d_gated = d_gated.reshape(length, HEADS, HEAD).transpose(1, 0, 2)
    d_gate = d_gated * normed
    d_attended = norm_back(d_gated * gate_part.astype(jnp.float32), normed, inverse).astype(jnp.bfloat16)
    d_query, d_key, d_value = lax.map(lambda stacked: head_backward(stacked[0], stacked[1], stacked[2], stacked[3]), (queries, key_heads, values, d_attended))
    d_project = jnp.stack([d_gate, d_value, d_query, d_key], 0).transpose(2, 1, 0, 3).reshape(length, 4 * HEADS * HEAD)
    d_before = (d_project * silu_slope(before)).astype(jnp.bfloat16)
    grad_heads = jnp.dot(x_low.T, d_before, preferred_element_type=jnp.float32)
    d_normed = jnp.dot(d_before, head_weights.T, preferred_element_type=jnp.float32)
    history_grad = d_layer + norm_back(d_normed, x_normed, x_inverse)
    return (losses, history_grad, grad_heads, grad_merge)
```

```python
import jax
import jax.numpy as jnp
from jax import lax
from jax.sharding import PartitionSpec as P

HEAD = 128
norm_eps = 1e-05
F32 = jnp.float32
BF16 = jnp.bfloat16


def sigmoid_slope(argument):
    part = jax.nn.sigmoid(argument)
    return argument * part, part * (1.0 + argument * (1.0 - part))


def layer_norm(argument):
    centred = argument - jnp.mean(argument, -1, keepdims=True)
    inverse = lax.rsqrt(jnp.mean(centred * centred, -1, keepdims=True) + norm_eps)
    return (centred * inverse, inverse)


def norm_back(gradient, normed, inverse):
    return inverse * (
        gradient
        - jnp.mean(gradient, -1, keepdims=True)
        - normed * jnp.mean(gradient * normed, -1, keepdims=True)
    )


def mm(left, right, dims=((1,), (0,))):
    return lax.dot_general(left, right, (dims, ((), ())), preferred_element_type=F32)


def mm_split(left, right, dims=((1,), (0,))):
    high = left.astype(BF16)
    rest = left - high.astype(F32)
    middle = rest.astype(BF16)
    low = (rest - middle.astype(F32)).astype(BF16)
    count = left.shape[0]
    product = mm(jnp.concatenate([high, middle, low], 0), right, dims)
    return product[:count] + product[count : 2 * count] + product[2 * count :]


def swap(block, axis):
    return lax.all_to_all(block, axis, 0, 0, tiled=True)


def send_all(block, axis, size):
    return swap(jnp.broadcast_to(block[None], (size,) + block.shape), axis)


def per_device(
    n_ctx,
    n_cand,
    history,
    head_weights,
    merge_weights,
    cand_table,
    user_weights,
    item_weights,
    score_weights,
    request_points,
    candidate_owner,
    candidate_row,
    relevance,
):
    rows, width = history.shape
    requests = request_points.shape[0]
    own = requests // n_ctx
    features = width * n_cand
    hidden = user_weights.shape[1]
    table_rows = cand_table.shape[0]
    strip = features // n_ctx
    ctx = lax.axis_index("ctx")
    cand = lax.axis_index("cand")
    first_row = ctx * rows
    scaling = HEAD ** (-0.5)

    item_proj = mm(cand_table, item_weights).astype(BF16)
    packed = jnp.concatenate(
        [merge_weights[:, :hidden], merge_weights[:, hidden:], user_weights, item_proj], 0
    )
    pack_rows = packed.shape[0]
    table = lax.all_gather(packed, "cand", axis=0, tiled=True)

    positions = first_row + jnp.arange(rows, dtype=jnp.int32)
    matches = (request_points[:, None] == positions[None, :]).astype(BF16)
    picked = mm(matches, history).astype(BF16).reshape(n_ctx, own, width)
    picked = swap(picked, "ctx")
    picked = jnp.sum(picked.astype(F32), 0).astype(BF16)

    pad = jnp.zeros((8 - own, width), BF16)
    both = lax.all_gather(
        jnp.concatenate([history, picked, pad], 0), "cand", axis=1, tiled=True
    )
    x_wide = both.astype(F32)
    x_normed, x_inverse = layer_norm(x_wide)
    x_low = x_normed.astype(BF16)
    before = mm(x_low, head_weights)
    smooth, slope = sigmoid_slope(before)
    project = smooth.astype(BF16)
    values = project[:rows, HEAD : 2 * HEAD]
    key_heads = project[:rows, 3 * HEAD :]
    gate = project[rows : rows + own, :HEAD].astype(F32)
    own_queries = project[rows : rows + own, 2 * HEAD : 3 * HEAD]
    request_low = x_low[rows : rows + own]

    queries = send_all(own_queries, "ctx", n_ctx).reshape(requests, HEAD)
    logits = mm(queries, key_heads, ((1,), (1,))) * scaling
    allowed = positions[None, :] <= request_points[:, None]
    divisor = (request_points + 1).astype(F32)[:, None]
    logit_smooth, logit_slope = sigmoid_slope(logits)
    weight = jnp.where(allowed, logit_smooth / divisor, 0.0).astype(BF16)
    attended = swap(mm(weight, values).reshape(n_ctx, own, HEAD), "ctx")
    attended = jnp.sum(attended, 0)
    normed, inverse = layer_norm(attended)
    gated = (normed * gate).astype(BF16)

    gated_full = send_all(gated, "cand", n_cand)
    gated_full = gated_full.transpose(1, 0, 2).reshape(own, features)
    blocks = table.reshape(n_cand, pack_rows, hidden)
    merge_left = blocks[:, :HEAD].reshape(features, hidden)
    merge_right = blocks[:, HEAD : 2 * HEAD].reshape(features, hidden)
    user_full = blocks[:, 2 * HEAD : 2 * HEAD + width].reshape(features, hidden)
    merged = jnp.concatenate([mm(gated_full, merge_left), mm(gated_full, merge_right)], 1)
    layer_out = (x_wide[rows : rows + own] + merged).astype(BF16)
    user_proj = mm(layer_out, user_full)

    place = candidate_owner * pack_rows + (pack_rows - table_rows) + candidate_row
    items = table[place].astype(F32)
    pre_score = user_proj[:, None, :] + items
    pre_smooth, pre_slope = sigmoid_slope(pre_score)
    scores = jnp.sum(pre_smooth * score_weights, -1)
    log_total = jnp.log(jnp.sum(jnp.exp(scores), -1, keepdims=True))
    target = (relevance + 1).astype(F32)
    target = target / jnp.sum(target, -1, keepdims=True)
    losses = log_total[:, 0] - jnp.sum(target * scores, -1)
    d_score = jnp.exp(scores - log_total) - target
    d_user = jnp.sum(d_score[:, :, None] * pre_slope, 1) * score_weights
    d_picked = mm_split(d_user, user_full, ((1,), (1,)))
    d_gated = mm_split(d_picked, merge_weights, ((1,), (1,)))
    d_attended = norm_back(d_gated * gate, normed, inverse).astype(BF16)
    d_before_gate = (d_gated * normed * slope[rows : rows + own, :HEAD]).astype(BF16)

    strips = jnp.concatenate(
        [
            request_low.reshape(own, n_ctx, strip),
            d_picked.astype(BF16).reshape(own, n_ctx, strip),
        ],
        2,
    ).transpose(1, 0, 2)
    strips = jnp.pad(strips, ((0, 0), (0, 0), (0, HEAD - 2 * strip)))
    shared = jnp.concatenate([d_attended, gated, d_before_gate], 0)
    sent = jnp.concatenate(
        [jnp.broadcast_to(shared[None], (n_ctx,) + shared.shape), strips], 1
    )
    sent = swap(sent, "ctx")
    all_grads = sent[:, :own].reshape(requests, HEAD)
    all_gated = sent[:, own : 2 * own].reshape(requests, HEAD)
    all_gate_grads = sent[:, 2 * own : 3 * own].reshape(requests, HEAD)
    all_strips = sent[:, 3 * own :].reshape(requests, HEAD)
    x_strip = all_strips[:, :strip]
    d_strip = all_strips[:, strip : 2 * strip]
    grad_merge = mm(all_gated, d_strip, ((0,), (0,)))
    slopes = mm(all_grads, values, ((1,), (1,)))
    d_logit = jnp.where(allowed, slopes * logit_slope / divisor, 0.0).astype(BF16)
    d_query = (mm(d_logit, key_heads) * scaling).astype(BF16)
    d_key = mm(d_logit, queries, ((0,), (0,))) * scaling
    d_value = mm(weight, all_grads, ((0,), (0,)))
    d_value = (d_value * slope[:rows, HEAD : 2 * HEAD]).astype(BF16)
    d_key = (d_key * slope[:rows, 3 * HEAD :]).astype(BF16)
    dense = jnp.concatenate([d_value, d_key], 1)
    dense_grad = mm(x_low[:rows], dense, ((0,), (0,))).astype(BF16)
    dense_grad = dense_grad.reshape(n_ctx, strip, 2 * HEAD)
    dense_grad = jnp.concatenate(
        [dense_grad[:, :, :HEAD], dense_grad[:, :, HEAD:], d_query.reshape(n_ctx, own, HEAD)], 1
    )
    dense_grad = jnp.sum(swap(dense_grad, "ctx").astype(F32), 0)
    own_query_grad = dense_grad[2 * strip :]
    d_before_query = (own_query_grad * slope[rows : rows + own, 2 * HEAD : 3 * HEAD]).astype(BF16)

    weights_dense = jnp.concatenate(
        [head_weights[:, HEAD : 2 * HEAD], head_weights[:, 3 * HEAD :]], 1
    )
    weights_request = jnp.concatenate(
        [head_weights[:, :HEAD], head_weights[:, 2 * HEAD : 3 * HEAD]], 1
    )
    request_before = jnp.concatenate([d_before_gate, d_before_query], 1)
    back_dense = norm_back(
        mm(dense, weights_dense, ((1,), (1,))), x_normed[:rows], x_inverse[:rows]
    )
    back_request = norm_back(
        mm(request_before, weights_request, ((1,), (1,))),
        x_normed[rows : rows + own],
        x_inverse[rows : rows + own],
    )
    back = jnp.concatenate(
        [back_dense, back_request, jnp.zeros((8 - own, features), F32)], 0
    ).astype(BF16)
    back = back.reshape(rows + 8, n_cand, width).transpose(1, 0, 2)
    back = jnp.sum(swap(back, "cand").astype(F32), 0)
    own_slice = lax.dynamic_slice_in_dim(d_picked, cand * width, width, 1)
    request_grad = back[rows : rows + own] + own_slice
    final = jnp.concatenate([request_grad.astype(BF16), d_before_query], 0)
    final = send_all(final, "ctx", n_ctx)
    all_request_grad = final[:, :own].reshape(requests, width)
    all_query_grads = final[:, own:].reshape(requests, HEAD)
    history_grad = back[:rows] + mm(matches, all_request_grad, ((0,), (0,)))
    gate_query = mm(
        x_strip, jnp.concatenate([all_gate_grads, all_query_grads], 1), ((0,), (0,))
    )
    grad_heads = jnp.concatenate(
        [
            gate_query[:, :HEAD],
            dense_grad[:strip],
            gate_query[:, HEAD:],
            dense_grad[strip : 2 * strip],
        ],
        1,
    )
    return (losses, history_grad, grad_heads, grad_merge)


def solution(mesh):
    n_ctx = mesh.shape["ctx"]
    n_cand = mesh.shape["cand"]

    def body(*args):
        return per_device(n_ctx, n_cand, *args)

    return jax.shard_map(
        body,
        mesh=mesh,
        in_specs=(
            P("ctx", "cand"),
            P(None, "cand"),
            P("cand", None),
            P("cand", None),
            P("cand", None),
            P(),
            P(),
            P(),
            P("ctx", None),
            P("ctx", None),
            P("ctx", None),
        ),
        out_specs=(P("ctx"), P("ctx", "cand"), P("ctx", "cand"), P("cand", "ctx")),
        check_vma=False,
    )
```

```python
import functools

import jax
import jax.numpy as jnp
from jax import lax
from jax.experimental import pallas as pl
from jax.experimental.pallas import tpu as pltpu
from jax.sharding import PartitionSpec as P

HEAD = 128
norm_eps = 1e-05
F32 = jnp.float32
BF16 = jnp.bfloat16
PAD = 16
CHUNK = 128


def sigmoid_slope(argument):
    part = jax.nn.sigmoid(argument)
    return argument * part, part * (1.0 + argument * (1.0 - part))


def layer_norm(argument):
    centred = argument - jnp.mean(argument, -1, keepdims=True)
    inverse = lax.rsqrt(jnp.mean(centred * centred, -1, keepdims=True) + norm_eps)
    return (centred * inverse, inverse)


def norm_back(gradient, normed, inverse):
    return inverse * (
        gradient
        - jnp.mean(gradient, -1, keepdims=True)
        - normed * jnp.mean(gradient * normed, -1, keepdims=True)
    )


def mm(left, right, dims=((1,), (0,))):
    return lax.dot_general(left, right, (dims, ((), ())), preferred_element_type=F32)


def mm_split(left, right, dims=((1,), (0,))):
    high = left.astype(BF16)
    rest = left - high.astype(F32)
    middle = rest.astype(BF16)
    low = (rest - middle.astype(F32)).astype(BF16)
    count = left.shape[0]
    product = mm(jnp.concatenate([high, middle, low], 0), right, dims)
    return product[:count] + product[count : 2 * count] + product[2 * count :]


def swap(block, axis):
    return lax.all_to_all(block, axis, 0, 0, tiled=True)


def send_all(block, axis, size):
    return swap(jnp.broadcast_to(block[None], (size,) + block.shape), axis)


def score_kernel(
    count,
    request_ref,
    gated_ref,
    merge_ref,
    user_ref,
    item_ref,
    weight_ref,
    owner_ref,
    row_ref,
    target_ref,
    cand_ref,
    out_ref,
    user_proj,
):
    heads = gated_ref.shape[0]
    gated = jnp.concatenate([gated_ref[head] for head in range(heads)], 1)
    layer_out = request_ref[...].astype(F32) + mm(gated, merge_ref[...])
    user_proj[...] = mm(layer_out.astype(BF16), user_ref[...])
    slots, hidden = owner_ref.shape[0], user_ref.shape[1]
    table_rows = item_ref.shape[0]
    weights = weight_ref[...]
    out_ref[...] = jnp.zeros_like(out_ref)
    lanes = lax.broadcasted_iota(jnp.int32, (CHUNK, table_rows), 1)
    for request in range(count):
        user_row = user_proj[request : request + 1, :]

        def step(index, sums, request=request, user_row=user_row):
            begin = pl.multiple_of(index * CHUNK, CHUNK)
            owned = owner_ref[pl.ds(begin, CHUNK), request : request + 1] == cand_ref[0]
            place = row_ref[pl.ds(begin, CHUNK), request : request + 1]
            target = target_ref[pl.ds(begin, CHUNK), request : request + 1]
            chosen = jnp.where(lanes == place, 1.0, 0.0).astype(BF16)
            pre_score = mm(chosen, item_ref[...]) + user_row
            part = 0.5 + 0.5 * jnp.tanh(0.5 * pre_score)
            smooth = pre_score * part
            slope = part + smooth * (1.0 - part)
            scores = jnp.sum(smooth * weights, -1, keepdims=True)
            power = jnp.where(owned, jnp.exp(scores), 0.0)
            target = jnp.where(owned, target, 0.0)
            soft = (0.25 * power * slope).reshape(-1, 8, hidden)
            hard = (target * slope).reshape(-1, 8, hidden)
            scalars = jnp.where(
                lax.broadcasted_iota(jnp.int32, (CHUNK, HEAD), 1) == 0, power, target * scores
            )
            return (
                sums[0] + jnp.sum(soft, 0),
                sums[1] + jnp.sum(hard, 0),
                sums[2] + jnp.sum(scalars.reshape(-1, 8, HEAD), 0),
            )

        zero = jnp.zeros((8, hidden), F32)
        sums = lax.fori_loop(
            0, slots // CHUNK, step, (zero, zero, jnp.zeros((8, HEAD), F32)), unroll=2
        )
        out_ref[request : request + 1, :hidden] = jnp.sum(sums[0], 0, keepdims=True)
        out_ref[request : request + 1, hidden : 2 * hidden] = jnp.sum(sums[1], 0, keepdims=True)
        out_ref[request : request + 1, 2 * hidden :] = jnp.sum(sums[2], 0, keepdims=True)


def score_parts(count, cand, request_rows, gated, merge, user, items, weights, owner, row, target):
    vmem = pl.BlockSpec(memory_space=pltpu.VMEM)
    hidden = user.shape[1]
    return pl.pallas_call(
        functools.partial(score_kernel, count),
        out_shape=jax.ShapeDtypeStruct((8, 2 * hidden + HEAD), F32),
        in_specs=[vmem] * 9 + [pl.BlockSpec(memory_space=pltpu.SMEM)],
        out_specs=vmem,
        scratch_shapes=[pltpu.VMEM((PAD, hidden), F32)],
        compiler_params=pltpu.CompilerParams(vmem_limit_bytes=48 * 1024 * 1024),
        cost_estimate=pl.CostEstimate(
            flops=3 * 10**9, bytes_accessed=5 * 10**6, transcendentals=10**6
        ),
    )(request_rows, gated, merge, user, items, weights, owner, row, target, cand)


def per_device(
    n_ctx,
    n_cand,
    history,
    head_weights,
    merge_weights,
    cand_table,
    user_weights,
    item_weights,
    score_weights,
    request_points,
    candidate_owner,
    candidate_row,
    relevance,
):
    rows, width = history.shape
    requests = request_points.shape[0]
    own = requests // n_ctx
    features = width * n_cand
    hidden = user_weights.shape[1]
    strip = features // n_ctx
    ctx = lax.axis_index("ctx")
    cand = lax.axis_index("cand")
    first_row = ctx * rows
    scaling = HEAD ** (-0.5)

    riding = lax.all_gather(
        jnp.concatenate([history, user_weights], 1), "cand", axis=0, tiled=False
    )
    merge_full = lax.all_gather(merge_weights, "cand", axis=0, tiled=True)

    positions = first_row + jnp.arange(rows, dtype=jnp.int32)
    matches = (request_points[:, None] == positions[None, :]).astype(BF16)
    picked = mm(matches, history).astype(BF16).reshape(n_ctx, own, width)
    picked = swap(picked, "ctx")
    picked = jnp.sum(picked.astype(F32), 0).astype(BF16)

    picked = send_all(jnp.pad(picked, ((0, PAD - own), (0, 0))), "cand", n_cand)
    picked = picked.transpose(1, 0, 2).reshape(PAD, features)
    r_normed, r_inverse = layer_norm(picked.astype(F32))
    request_low = r_normed.astype(BF16)
    weights_request = jnp.concatenate(
        [head_weights[:, :HEAD], head_weights[:, 2 * HEAD : 3 * HEAD]], 1
    )
    before_request = mm(request_low, weights_request)
    smooth, slope_request = sigmoid_slope(before_request)
    gate = smooth[:own, :HEAD].astype(BF16).astype(F32)
    own_queries = smooth[:own, HEAD:].astype(BF16)

    x_wide = riding[:, :, :width].transpose(1, 0, 2).reshape(rows, features).astype(F32)
    user_full = riding[:, :, width:].reshape(features, hidden)
    x_normed, x_inverse = layer_norm(x_wide)
    x_low = x_normed.astype(BF16)
    weights_dense = jnp.concatenate(
        [head_weights[:, HEAD : 2 * HEAD], head_weights[:, 3 * HEAD :]], 1
    )
    before = mm(x_low, weights_dense)
    smooth, slope = sigmoid_slope(before)
    values = smooth[:, :HEAD].astype(BF16)
    key_heads = smooth[:, HEAD:].astype(BF16)

    queries = send_all(own_queries, "ctx", n_ctx).reshape(requests, HEAD)
    logits = mm(queries, key_heads, ((1,), (1,))) * scaling
    allowed = positions[None, :] <= request_points[:, None]
    divisor = (request_points + 1).astype(F32)[:, None]
    logit_smooth, logit_slope = sigmoid_slope(logits)
    weight = jnp.where(allowed, logit_smooth / divisor, 0.0).astype(BF16)
    attended = swap(mm(weight, values).reshape(n_ctx, own, HEAD), "ctx")
    attended = jnp.sum(attended, 0)
    normed, inverse = layer_norm(attended)
    gated = (normed * gate).astype(BF16)

    item_proj = mm(cand_table, item_weights).astype(BF16)
    target = (relevance + 1).astype(F32)
    target = target / jnp.sum(target, -1, keepdims=True)
    gated, merge_full, user_full = lax.optimization_barrier((gated, merge_full, user_full))
    gated_full = send_all(jnp.pad(gated, ((0, PAD - own), (0, 0))), "cand", n_cand)
    parts = score_parts(
        own,
        cand[None],
        picked,
        gated_full,
        merge_full,
        user_full,
        item_proj,
        score_weights[None],
        candidate_owner.T,
        candidate_row.T,
        target.T,
    )
    parts = jnp.sum(send_all(parts[:own], "cand", n_cand).reshape(n_cand, own, -1), 0)
    total = parts[:, 2 * hidden : 2 * hidden + 1]
    losses = jnp.log(total[:, 0]) - parts[:, 2 * hidden + 1]
    d_user = parts[:, :hidden] / (0.25 * total) - parts[:, hidden : 2 * hidden]
    d_user = d_user * score_weights
    d_picked = mm_split(d_user, user_full, ((1,), (1,)))
    d_gated = mm_split(d_picked, merge_weights, ((1,), (1,)))
    d_attended = norm_back(d_gated * gate, normed, inverse).astype(BF16)
    d_before_gate = (d_gated * normed * slope_request[:own, :HEAD]).astype(BF16)

    blocks = features // HEAD
    strips = jnp.concatenate(
        [
            request_low[:own].reshape(own, blocks, HEAD).transpose(1, 0, 2),
            d_picked.astype(BF16).reshape(own, blocks, HEAD).transpose(1, 0, 2),
        ],
        1,
    )
    strips = jnp.repeat(strips, n_ctx // blocks, axis=0)
    shared = jnp.concatenate([d_attended, gated, d_before_gate], 0)
    sent = jnp.concatenate(
        [jnp.broadcast_to(shared[None], (n_ctx,) + shared.shape), strips], 1
    )
    sent = swap(sent, "ctx")
    all_grads = sent[:, :own].reshape(requests, HEAD)
    all_gated = sent[:, own : 2 * own].reshape(requests, HEAD)
    all_gate_grads = sent[:, 2 * own : 3 * own].reshape(requests, HEAD)
    x_block = sent[:, 3 * own : 4 * own].reshape(requests, HEAD)
    d_block = sent[:, 4 * own :].reshape(requests, HEAD)
    lane = lax.rem(ctx, n_ctx // blocks) * strip
    grad_merge = mm(d_block, all_gated, ((0,), (0,)))
    grad_merge = lax.dynamic_slice_in_dim(grad_merge, lane, strip, 0).T
    slopes = mm(all_grads, values, ((1,), (1,)))
    d_logit = jnp.where(allowed, slopes * logit_slope / divisor, 0.0).astype(BF16)
    d_query = (mm(d_logit, key_heads) * scaling).astype(BF16)
    d_key = mm(d_logit, queries, ((0,), (0,))) * scaling
    d_value = mm(weight, all_grads, ((0,), (0,)))
    d_value = (d_value * slope[:, :HEAD]).astype(BF16)
    d_key = (d_key * slope[:, HEAD:]).astype(BF16)
    dense = jnp.concatenate([d_value, d_key], 1)
    dense_grad = mm(x_low, dense, ((0,), (0,))).astype(BF16)
    dense_grad = dense_grad.reshape(n_ctx, strip, 2 * HEAD)
    dense_grad = jnp.concatenate(
        [dense_grad[:, :, :HEAD], dense_grad[:, :, HEAD:], d_query.reshape(n_ctx, own, HEAD)], 1
    )
    dense_grad = jnp.sum(swap(dense_grad, "ctx").astype(F32), 0)
    own_query_grad = dense_grad[2 * strip :]
    d_before_query = (own_query_grad * slope_request[:own, HEAD:]).astype(BF16)

    back_dense = norm_back(mm(dense, weights_dense, ((1,), (1,))), x_normed, x_inverse)
    back_dense = lax.psum_scatter(
        back_dense.reshape(rows, n_cand, width).transpose(1, 0, 2).reshape(n_cand * rows, width),
        "cand",
        scatter_dimension=0,
        tiled=True,
    )
    request_before = jnp.concatenate([d_before_gate, d_before_query], 1)
    back = norm_back(
        mm(request_before, weights_request, ((1,), (1,))), r_normed[:own], r_inverse[:own]
    )
    back = back.reshape(own, n_cand, width).transpose(1, 0, 2)
    back = jnp.sum(swap(back, "cand"), 0)
    own_slice = lax.dynamic_slice_in_dim(d_picked, cand * width, width, 1)
    request_grad = back + own_slice
    final = jnp.concatenate([request_grad.astype(BF16), d_before_query], 0)
    final = send_all(final, "ctx", n_ctx)
    all_request_grad = final[:, :own].reshape(requests, width)
    all_query_grads = final[:, own:].reshape(requests, HEAD)
    history_grad = back_dense + mm(matches, all_request_grad, ((0,), (0,)))
    gate_query = mm(
        x_block, jnp.concatenate([all_gate_grads, all_query_grads], 1), ((0,), (0,))
    )
    gate_query = lax.dynamic_slice_in_dim(gate_query, lane, strip, 0)
    grad_heads = jnp.concatenate(
        [
            gate_query[:, :HEAD],
            dense_grad[:strip],
            gate_query[:, HEAD:],
            dense_grad[strip : 2 * strip],
        ],
        1,
    )
    return (losses, history_grad, grad_heads, grad_merge)


def solution(mesh):
    n_ctx = mesh.shape["ctx"]
    n_cand = mesh.shape["cand"]

    def body(*args):
        return per_device(n_ctx, n_cand, *args)

    return jax.shard_map(
        body,
        mesh=mesh,
        in_specs=(
            P("ctx", "cand"),
            P(None, "cand"),
            P("cand", None),
            P("cand", None),
            P("cand", None),
            P(),
            P(),
            P(),
            P("ctx", None),
            P("ctx", None),
            P("ctx", None),
        ),
        out_specs=(P("ctx"), P("ctx", "cand"), P("ctx", "cand"), P("cand", "ctx")),
        check_vma=False,
    )
```

```python
import functools

import jax
import jax.numpy as jnp
from jax import lax
from jax.experimental import pallas as pl
from jax.experimental.pallas import tpu as pltpu
from jax.sharding import PartitionSpec as P

HEAD = 128
norm_eps = 1e-05
F32 = jnp.float32
BF16 = jnp.bfloat16
PAD = 16
CHUNK = 128


def sigmoid_slope(argument):
    part = jax.nn.sigmoid(argument)
    return argument * part, part * (1.0 + argument * (1.0 - part))


def layer_norm(argument):
    centred = argument - jnp.mean(argument, -1, keepdims=True)
    inverse = lax.rsqrt(jnp.mean(centred * centred, -1, keepdims=True) + norm_eps)
    return (centred * inverse, inverse)


def norm_back(gradient, normed, inverse):
    return inverse * (
        gradient
        - jnp.mean(gradient, -1, keepdims=True)
        - normed * jnp.mean(gradient * normed, -1, keepdims=True)
    )


def mm(left, right, dims=((1,), (0,))):
    return lax.dot_general(left, right, (dims, ((), ())), preferred_element_type=F32)


def mm_split(left, right, dims=((1,), (0,))):
    high = left.astype(BF16)
    rest = left - high.astype(F32)
    middle = rest.astype(BF16)
    low = (rest - middle.astype(F32)).astype(BF16)
    count = left.shape[0]
    product = mm(jnp.concatenate([high, middle, low], 0), right, dims)
    return product[:count] + product[count : 2 * count] + product[2 * count :]


def swap(block, axis):
    return lax.all_to_all(block, axis, 0, 0, tiled=True)


def send_all(block, axis, size):
    return swap(jnp.broadcast_to(block[None], (size,) + block.shape), axis)


def select_kernel(first_ref, points_ref, history_ref, user_ref, picked_ref, joined_ref):
    rows, requests = history_ref.shape[0], points_ref.shape[1]
    positions = lax.broadcasted_iota(jnp.int32, (rows, requests), 0) + first_ref[0]
    matches = jnp.where(positions == points_ref[...], 1.0, 0.0).astype(BF16)
    picked = mm(matches, history_ref[...], ((0,), (0,)))
    picked_ref[...] = picked.astype(BF16)
    joined_ref[:, : history_ref.shape[1]] = history_ref[...]
    joined_ref[:, history_ref.shape[1] :] = user_ref[...]


def select_rows(first_row, points, history, user):
    vmem = pl.BlockSpec(memory_space=pltpu.VMEM)
    rows, width = history.shape
    return pl.pallas_call(
        select_kernel,
        out_shape=(
            jax.ShapeDtypeStruct((points.shape[0], width), BF16),
            jax.ShapeDtypeStruct((rows, width + user.shape[1]), BF16),
        ),
        in_specs=[pl.BlockSpec(memory_space=pltpu.SMEM)] + [vmem] * 3,
        out_specs=(vmem, vmem),
    )(first_row[None], points[None], history, user)


def score_kernel(
    count,
    request_ref,
    gated_ref,
    merge_ref,
    user_ref,
    items_hbm,
    weight_ref,
    owner_ref,
    target_ref,
    cand_ref,
    out_ref,
    user_proj,
    items_ref,
    item_sems,
):
    heads = gated_ref.shape[0]
    slots, hidden = owner_ref.shape[0], user_ref.shape[1]
    item_copies = [
        pltpu.make_async_copy(
            items_hbm.at[pl.ds(request * slots, slots)],
            items_ref.at[pl.ds(request * slots, slots)],
            item_sems.at[request],
        )
        for request in range(count)
    ]
    for copy in item_copies:
        copy.start()
    gated = jnp.concatenate([gated_ref[head] for head in range(heads)], 1)
    layer_out = request_ref[...].astype(F32) + mm(gated, merge_ref[...])
    user_proj[...] = 0.5 * mm(layer_out.astype(BF16), user_ref[...])
    weights = weight_ref[...]
    for request in range(count):
        user_row = user_proj[request : request + 1, :]
        item_copies[request].wait()

        def step(index, sums, request=request, user_row=user_row):
            begin = pl.multiple_of(index * CHUNK, CHUNK)
            owned = owner_ref[pl.ds(begin, CHUNK), request : request + 1] == cand_ref[0]
            target = target_ref[pl.ds(begin, CHUNK), request : request + 1]
            items = items_ref[pl.ds(request * slots + begin, CHUNK), :]
            half = items.astype(F32) + user_row
            above = 1.0 + jnp.tanh(half)
            smooth = half * above
            slope = above * ((half + half + 1.0) - smooth)
            scores = jnp.sum(smooth * weights, -1, keepdims=True)
            power = jnp.where(owned, jnp.exp(scores), 0.0)
            target = jnp.where(owned, target, 0.0)
            soft = ((0.125 * power) * slope).reshape(-1, 8, hidden)
            hard = ((0.5 * target) * slope).reshape(-1, 8, hidden)
            scalars = jnp.where(
                lax.broadcasted_iota(jnp.int32, (CHUNK, HEAD), 1) == 0, power, target * scores
            )
            return (
                sums[0] + jnp.sum(soft, 0),
                sums[1] + jnp.sum(hard, 0),
                sums[2] + jnp.sum(scalars.reshape(-1, 8, HEAD), 0),
            )

        zero = jnp.zeros((8, hidden), F32)
        sums = lax.fori_loop(
            0, slots // CHUNK, step, (zero, zero, jnp.zeros((8, HEAD), F32)), unroll=2
        )
        out_ref[request : request + 1, :hidden] = jnp.sum(sums[0], 0, keepdims=True)
        out_ref[request : request + 1, hidden : 2 * hidden] = jnp.sum(sums[1], 0, keepdims=True)
        out_ref[request : request + 1, 2 * hidden :] = jnp.sum(sums[2], 0, keepdims=True)


def score_parts(count, cand, request_rows, gated, merge, user, items, weights, owner, target):
    vmem = pl.BlockSpec(memory_space=pltpu.VMEM)
    hidden = user.shape[1]
    return pl.pallas_call(
        functools.partial(score_kernel, count),
        out_shape=jax.ShapeDtypeStruct((count, 2 * hidden + HEAD), F32),
        in_specs=[vmem] * 4
        + [pl.BlockSpec(memory_space=pltpu.HBM)]
        + [vmem] * 3
        + [pl.BlockSpec(memory_space=pltpu.SMEM)],
        out_specs=vmem,
        scratch_shapes=[
            pltpu.VMEM((PAD, hidden), F32),
            pltpu.VMEM(items.shape, BF16),
            pltpu.SemaphoreType.DMA((count,)),
        ],
        compiler_params=pltpu.CompilerParams(vmem_limit_bytes=16 * 1024 * 1024),
        cost_estimate=pl.CostEstimate(
            flops=10**8, bytes_accessed=5 * 10**6, transcendentals=10**6
        ),
    )(request_rows, gated, merge, user, items, weights, owner, target, cand)


def per_device(
    n_ctx,
    n_cand,
    history,
    head_weights,
    merge_weights,
    cand_table,
    user_weights,
    item_weights,
    score_weights,
    request_points,
    candidate_owner,
    candidate_row,
    relevance,
):
    rows, width = history.shape
    requests = request_points.shape[0]
    own = requests // n_ctx
    features = width * n_cand
    hidden = user_weights.shape[1]
    strip = features // n_ctx
    ctx = lax.axis_index("ctx")
    cand = lax.axis_index("cand")
    first_row = ctx * rows
    scaling = HEAD ** (-0.5)

    picked, joined = select_rows(first_row, request_points, history, user_weights)
    riding = lax.all_gather(joined, "cand", axis=0, tiled=False)
    merge_full = lax.all_gather(merge_weights, "cand", axis=0, tiled=True)
    positions = first_row + jnp.arange(rows, dtype=jnp.int32)
    matches = (request_points[:, None] == positions[None, :]).astype(BF16)
    picked = picked.reshape(n_ctx, own, width)
    picked = swap(picked, "ctx")
    picked = jnp.sum(picked.astype(F32), 0).astype(BF16)

    picked = send_all(jnp.pad(picked, ((0, PAD - own), (0, 0))), "cand", n_cand)
    picked = picked.transpose(1, 0, 2).reshape(PAD, features)
    r_normed, r_inverse = layer_norm(picked.astype(F32))
    request_low = r_normed.astype(BF16)
    weights_request = jnp.concatenate(
        [head_weights[:, :HEAD], head_weights[:, 2 * HEAD : 3 * HEAD]], 1
    )
    before_request = mm(request_low, weights_request)
    smooth, slope_request = sigmoid_slope(before_request)
    gate = smooth[:own, :HEAD].astype(BF16).astype(F32)
    own_queries = smooth[:own, HEAD:].astype(BF16)

    x_wide = riding[:, :, :width].transpose(1, 0, 2).reshape(rows, features).astype(F32)
    user_full = riding[:, :, width:].reshape(features, hidden)
    x_normed, x_inverse = layer_norm(x_wide)
    x_low = x_normed.astype(BF16)
    weights_dense = jnp.concatenate(
        [head_weights[:, HEAD : 2 * HEAD], head_weights[:, 3 * HEAD :]], 1
    )
    before = mm(x_low, weights_dense)
    smooth, slope = sigmoid_slope(before)
    values = smooth[:, :HEAD].astype(BF16)
    key_heads = smooth[:, HEAD:].astype(BF16)

    queries = send_all(own_queries, "ctx", n_ctx).reshape(requests, HEAD)
    logits = mm(queries, key_heads, ((1,), (1,))) * scaling
    allowed = positions[None, :] <= request_points[:, None]
    divisor = (request_points + 1).astype(F32)[:, None]
    logit_smooth, logit_slope = sigmoid_slope(logits)
    weight = jnp.where(allowed, logit_smooth / divisor, 0.0).astype(BF16)
    attended = mm(weight, values).astype(BF16).reshape(n_ctx, own, HEAD)
    candidate_row, attended = lax.optimization_barrier((candidate_row, attended))
    attended = jnp.sum(swap(attended, "ctx").astype(F32), 0)
    item_proj = (0.5 * mm(cand_table, item_weights)).astype(BF16)
    lanes = jnp.arange(item_proj.shape[0], dtype=jnp.int32)
    chosen = (candidate_row.reshape(-1)[:, None] == lanes[None, :]).astype(BF16)
    items = mm(chosen, item_proj).astype(BF16)
    normed, inverse = layer_norm(attended)
    gated = (normed * gate).astype(BF16)

    target = (relevance + 1).astype(F32)
    target = target / jnp.sum(target, -1, keepdims=True)
    gated, items = lax.optimization_barrier((gated, items))
    gated_full = send_all(jnp.pad(gated, ((0, PAD - own), (0, 0))), "cand", n_cand)
    parts = score_parts(
        own,
        cand[None],
        picked,
        gated_full,
        merge_full,
        user_full,
        items,
        score_weights[None],
        candidate_owner.T,
        target.T,
    )
    parts = jnp.sum(send_all(parts, "cand", n_cand).reshape(n_cand, own, -1), 0)
    total = parts[:, 2 * hidden : 2 * hidden + 1]
    losses = jnp.log(total[:, 0]) - parts[:, 2 * hidden + 1]
    d_user = parts[:, :hidden] / (0.25 * total) - parts[:, hidden : 2 * hidden]
    d_user = d_user * score_weights
    d_picked = mm_split(d_user, user_full, ((1,), (1,)))
    d_gated = mm_split(d_picked, merge_weights, ((1,), (1,)))
    d_attended = norm_back(d_gated * gate, normed, inverse).astype(BF16)
    d_before_gate = (d_gated * normed * slope_request[:own, :HEAD]).astype(BF16)

    blocks = features // HEAD

    def strips_of(wide):
        wide = wide.reshape(own, blocks, HEAD).transpose(1, 0, 2)
        return jnp.repeat(wide, n_ctx // blocks, axis=0)

    shared = jnp.concatenate([d_attended, gated, d_before_gate], 0)
    sent = jnp.concatenate(
        [
            jnp.broadcast_to(shared[None], (n_ctx,) + shared.shape),
            strips_of(d_picked.astype(BF16)),
        ],
        1,
    )
    sent = swap(sent, "ctx")
    all_grads = sent[:, :own].reshape(requests, HEAD)
    all_gated = sent[:, own : 2 * own].reshape(requests, HEAD)
    all_gate_grads = sent[:, 2 * own : 3 * own].reshape(requests, HEAD)
    d_block = sent[:, 3 * own :].reshape(requests, HEAD)
    lane = lax.rem(ctx, n_ctx // blocks) * strip
    grad_merge = mm(d_block, all_gated, ((0,), (0,)))
    grad_merge = lax.dynamic_slice_in_dim(grad_merge, lane, strip, 0).T
    slopes = mm(all_grads, values, ((1,), (1,)))
    d_logit = jnp.where(allowed, slopes * logit_slope / divisor, 0.0).astype(BF16)
    d_query = (mm(d_logit, key_heads) * scaling).astype(BF16)
    d_key = mm(d_logit, queries, ((0,), (0,))) * scaling
    d_value = mm(weight, all_grads, ((0,), (0,)))
    d_value = (d_value * slope[:, :HEAD]).astype(BF16)
    d_key = (d_key * slope[:, HEAD:]).astype(BF16)
    dense = jnp.concatenate([d_value, d_key], 1)
    dense_grad = mm(x_low, dense, ((0,), (0,))).astype(BF16)
    dense_grad = dense_grad.reshape(n_ctx, strip, 2 * HEAD)
    dense_grad = jnp.concatenate(
        [
            dense_grad[:, :, :HEAD],
            dense_grad[:, :, HEAD:],
            d_query.reshape(n_ctx, own, HEAD),
            strips_of(request_low[:own]),
        ],
        1,
    )
    dense_grad = swap(dense_grad, "ctx")
    x_block = dense_grad[:, 2 * strip + own :].reshape(requests, HEAD)
    dense_grad = jnp.sum(dense_grad[:, : 2 * strip + own].astype(F32), 0)
    own_query_grad = dense_grad[2 * strip :]
    d_before_query = (own_query_grad * slope_request[:own, HEAD:]).astype(BF16)

    back_dense = norm_back(mm(dense, weights_dense, ((1,), (1,))), x_normed, x_inverse)
    back_dense = lax.psum_scatter(
        back_dense.reshape(rows, n_cand, width).transpose(1, 0, 2).reshape(n_cand * rows, width),
        "cand",
        scatter_dimension=0,
        tiled=True,
    )
    request_before = jnp.concatenate([d_before_gate, d_before_query], 1)
    back = norm_back(
        mm(request_before, weights_request, ((1,), (1,))), r_normed[:own], r_inverse[:own]
    )
    back = back.reshape(own, n_cand, width).transpose(1, 0, 2)
    back = jnp.sum(swap(back, "cand"), 0)
    own_slice = lax.dynamic_slice_in_dim(d_picked, cand * width, width, 1)
    request_grad = back + own_slice
    final = jnp.concatenate([request_grad.astype(BF16), d_before_query], 0)
    final = send_all(final, "ctx", n_ctx)
    all_request_grad = final[:, :own].reshape(requests, width)
    all_query_grads = final[:, own:].reshape(requests, HEAD)
    history_grad = back_dense + mm(matches, all_request_grad, ((0,), (0,)))
    gate_query = mm(
        x_block, jnp.concatenate([all_gate_grads, all_query_grads], 1), ((0,), (0,))
    )
    gate_query = lax.dynamic_slice_in_dim(gate_query, lane, strip, 0)
    grad_heads = jnp.concatenate(
        [
            gate_query[:, :HEAD],
            dense_grad[:strip],
            gate_query[:, HEAD:],
            dense_grad[strip : 2 * strip],
        ],
        1,
    )
    return (losses, history_grad, grad_heads, grad_merge)


def solution(mesh):
    n_ctx = mesh.shape["ctx"]
    n_cand = mesh.shape["cand"]

    def body(*args):
        return per_device(n_ctx, n_cand, *args)

    return jax.shard_map(
        body,
        mesh=mesh,
        in_specs=(
            P("ctx", "cand"),
            P(None, "cand"),
            P("cand", None),
            P("cand", None),
            P("cand", None),
            P(),
            P(),
            P(),
            P("ctx", None),
            P("ctx", None),
            P("ctx", None),
        ),
        out_specs=(P("ctx"), P("ctx", "cand"), P("ctx", "cand"), P("cand", "ctx")),
        check_vma=False,
    )
```

```python
import functools

import jax
import jax.numpy as jnp
from jax import lax
from jax.experimental import pallas as pl
from jax.experimental.pallas import tpu as pltpu
from jax.sharding import PartitionSpec as P

HEAD = 128
norm_eps = 1e-05
F32 = jnp.float32
BF16 = jnp.bfloat16
PAD = 16
CHUNK = 64
UNROLL = 8


def sigmoid_slope(argument):
    part = jax.nn.sigmoid(argument)
    return argument * part, part * (1.0 + argument * (1.0 - part))


def layer_norm(argument):
    centred = argument - jnp.mean(argument, -1, keepdims=True)
    inverse = lax.rsqrt(jnp.mean(centred * centred, -1, keepdims=True) + norm_eps)
    return (centred * inverse, inverse)


def norm_back(gradient, normed, inverse):
    return inverse * (
        gradient
        - jnp.mean(gradient, -1, keepdims=True)
        - normed * jnp.mean(gradient * normed, -1, keepdims=True)
    )


def mm(left, right, dims=((1,), (0,))):
    return lax.dot_general(left, right, (dims, ((), ())), preferred_element_type=F32)


def mm_split(left, right, dims=((1,), (0,))):
    high = left.astype(BF16)
    rest = left - high.astype(F32)
    middle = rest.astype(BF16)
    low = (rest - middle.astype(F32)).astype(BF16)
    count = left.shape[0]
    product = mm(jnp.concatenate([high, middle, low], 0), right, dims)
    return product[:count] + product[count : 2 * count] + product[2 * count :]


def swap(block, axis):
    return lax.all_to_all(block, axis, 0, 0, tiled=True)


def send_all(block, axis, size):
    return swap(jnp.broadcast_to(block[None], (size,) + block.shape), axis)


def select_kernel(first_ref, points_ref, history_ref, user_ref, picked_ref, joined_ref):
    rows, requests = history_ref.shape[0], points_ref.shape[1]
    positions = lax.broadcasted_iota(jnp.int32, (rows, requests), 0) + first_ref[0]
    matches = jnp.where(positions == points_ref[...], 1.0, 0.0).astype(BF16)
    picked = mm(matches, history_ref[...], ((0,), (0,)))
    picked_ref[...] = picked.astype(BF16)
    joined_ref[:, : history_ref.shape[1]] = history_ref[...]
    joined_ref[:, history_ref.shape[1] :] = user_ref[...]


def select_rows(first_row, points, history, user):
    vmem = pl.BlockSpec(memory_space=pltpu.VMEM)
    rows, width = history.shape
    return pl.pallas_call(
        select_kernel,
        out_shape=(
            jax.ShapeDtypeStruct((points.shape[0], width), BF16),
            jax.ShapeDtypeStruct((rows, width + user.shape[1]), BF16),
        ),
        in_specs=[pl.BlockSpec(memory_space=pltpu.SMEM)] + [vmem] * 3,
        out_specs=(vmem, vmem),
    )(first_row[None], points[None], history, user)


def score_kernel(
    count,
    request_ref,
    gated_ref,
    merge_ref,
    user_ref,
    items_hbm,
    weight_ref,
    owner_ref,
    target_ref,
    cand_ref,
    out_ref,
    user_proj,
    items_ref,
    item_sems,
):
    heads = gated_ref.shape[0]
    slots, hidden = owner_ref.shape[0], user_ref.shape[1]
    item_copies = [
        pltpu.make_async_copy(
            items_hbm.at[pl.ds(request * slots, slots)],
            items_ref.at[pl.ds(request * slots, slots)],
            item_sems.at[request],
        )
        for request in range(count)
    ]
    for copy in item_copies:
        copy.start()
    gated = jnp.concatenate([gated_ref[head] for head in range(heads)], 1)
    layer_out = request_ref[...].astype(F32) + mm(gated, merge_ref[...])
    user_proj[...] = 0.5 * mm(layer_out.astype(BF16), user_ref[...])
    weights = weight_ref[...]
    for request in range(count):
        user_row = user_proj[request : request + 1, :]
        item_copies[request].wait()

        def step(index, sums, request=request, user_row=user_row):
            begin = pl.multiple_of(index * CHUNK, CHUNK)
            owned = owner_ref[pl.ds(begin, CHUNK), request : request + 1] == cand_ref[0]
            target = target_ref[pl.ds(begin, CHUNK), request : request + 1]
            items = items_ref[pl.ds(request * slots + begin, CHUNK), :]
            half = items.astype(F32) + user_row
            above = 1.0 + jnp.tanh(half)
            smooth = half * above
            slope = above * ((half + half + 1.0) - smooth)
            scores = jnp.sum(smooth * weights, -1, keepdims=True)
            power = jnp.where(owned, jnp.exp(scores), 0.0)
            target = jnp.where(owned, target, 0.0)
            soft = ((0.125 * power) * slope).reshape(-1, 8, hidden)
            hard = ((0.5 * target) * slope).reshape(-1, 8, hidden)
            scalars = jnp.where(
                lax.broadcasted_iota(jnp.int32, (CHUNK, HEAD), 1) == 0, power, target * scores
            )
            return (
                sums[0] + jnp.sum(soft, 0),
                sums[1] + jnp.sum(hard, 0),
                sums[2] + jnp.sum(scalars.reshape(-1, 8, HEAD), 0),
            )

        zero = jnp.zeros((8, hidden), F32)
        sums = lax.fori_loop(
            0, slots // CHUNK, step, (zero, zero, jnp.zeros((8, HEAD), F32)), unroll=UNROLL
        )
        out_ref[request : request + 1, :hidden] = jnp.sum(sums[0], 0, keepdims=True)
        out_ref[request : request + 1, hidden : 2 * hidden] = jnp.sum(sums[1], 0, keepdims=True)
        out_ref[request : request + 1, 2 * hidden :] = jnp.sum(sums[2], 0, keepdims=True)


def score_parts(count, cand, request_rows, gated, merge, user, items, weights, owner, target):
    vmem = pl.BlockSpec(memory_space=pltpu.VMEM)
    hidden = user.shape[1]
    return pl.pallas_call(
        functools.partial(score_kernel, count),
        out_shape=jax.ShapeDtypeStruct((count, 2 * hidden + HEAD), F32),
        in_specs=[vmem] * 4
        + [pl.BlockSpec(memory_space=pltpu.HBM)]
        + [vmem] * 3
        + [pl.BlockSpec(memory_space=pltpu.SMEM)],
        out_specs=vmem,
        scratch_shapes=[
            pltpu.VMEM((PAD, hidden), F32),
            pltpu.VMEM(items.shape, BF16),
            pltpu.SemaphoreType.DMA((count,)),
        ],
        compiler_params=pltpu.CompilerParams(vmem_limit_bytes=16 * 1024 * 1024),
        cost_estimate=pl.CostEstimate(
            flops=10**8, bytes_accessed=5 * 10**6, transcendentals=10**6
        ),
    )(request_rows, gated, merge, user, items, weights, owner, target, cand)


def per_device(
    n_ctx,
    n_cand,
    history,
    head_weights,
    merge_weights,
    cand_table,
    user_weights,
    item_weights,
    score_weights,
    request_points,
    candidate_owner,
    candidate_row,
    relevance,
):
    rows, width = history.shape
    requests = request_points.shape[0]
    own = requests // n_ctx
    features = width * n_cand
    hidden = user_weights.shape[1]
    strip = features // n_ctx
    ctx = lax.axis_index("ctx")
    cand = lax.axis_index("cand")
    first_row = ctx * rows
    scaling = HEAD ** (-0.5)

    picked, joined = select_rows(first_row, request_points, history, user_weights)
    riding = lax.all_gather(joined, "cand", axis=0, tiled=False)
    merge_full = lax.all_gather(merge_weights, "cand", axis=0, tiled=True)
    positions = first_row + jnp.arange(rows, dtype=jnp.int32)
    matches = (request_points[:, None] == positions[None, :]).astype(BF16)
    picked = picked.reshape(n_ctx, own, width)
    late_table, picked = lax.optimization_barrier((cand_table, picked))
    item_proj = (0.5 * mm(late_table, item_weights)).astype(BF16)
    picked = swap(picked, "ctx")
    picked = jnp.sum(picked.astype(F32), 0).astype(BF16)
    picked, item_proj = lax.optimization_barrier((picked, item_proj))

    picked = send_all(picked, "cand", n_cand).transpose(1, 0, 2).reshape(own, features)
    r_normed, r_inverse = layer_norm(picked.astype(F32))
    request_low = r_normed.astype(BF16)
    weights_request = jnp.concatenate(
        [head_weights[:, :HEAD], head_weights[:, 2 * HEAD : 3 * HEAD]], 1
    )
    before_request = mm(request_low, weights_request)
    smooth, slope_request = sigmoid_slope(before_request)
    gate = smooth[:own, :HEAD].astype(BF16).astype(F32)
    own_queries = smooth[:own, HEAD:].astype(BF16)

    x_wide = riding[:, :, :width].transpose(1, 0, 2).reshape(rows, features).astype(F32)
    user_full = riding[:, :, width:].reshape(features, hidden)
    x_normed, x_inverse = layer_norm(x_wide)
    x_low = x_normed.astype(BF16)
    weights_dense = jnp.concatenate(
        [head_weights[:, HEAD : 2 * HEAD], head_weights[:, 3 * HEAD :]], 1
    )
    before = mm(x_low, weights_dense)
    smooth, slope = sigmoid_slope(before)
    values = smooth[:, :HEAD].astype(BF16)
    key_heads = smooth[:, HEAD:].astype(BF16)

    queries = send_all(own_queries, "ctx", n_ctx).reshape(requests, HEAD)
    logits = mm(queries, key_heads, ((1,), (1,))) * scaling
    allowed = positions[None, :] <= request_points[:, None]
    divisor = (request_points + 1).astype(F32)[:, None]
    logit_smooth, logit_slope = sigmoid_slope(logits)
    weight = jnp.where(allowed, logit_smooth / divisor, 0.0).astype(BF16)
    attended = mm(weight, values).astype(BF16).reshape(n_ctx, own, HEAD)
    candidate_row, attended = lax.optimization_barrier((candidate_row, attended))
    attended = jnp.sum(swap(attended, "ctx").astype(F32), 0)
    lanes = jnp.arange(item_proj.shape[0], dtype=jnp.int32)
    chosen = (candidate_row.reshape(-1)[:, None] == lanes[None, :]).astype(BF16)
    items = mm(chosen, item_proj).astype(BF16)
    normed, inverse = layer_norm(attended)
    gated = (normed * gate).astype(BF16)

    target = (relevance + 1).astype(F32)
    target = target / jnp.sum(target, -1, keepdims=True)
    gated, items, user_full = lax.optimization_barrier((gated, items, user_full))
    gated_full = send_all(jnp.pad(gated, ((0, PAD - own), (0, 0))), "cand", n_cand)
    parts = score_parts(
        own,
        cand[None],
        jnp.pad(picked, ((0, PAD - own), (0, 0))),
        gated_full,
        merge_full,
        user_full,
        items,
        score_weights[None],
        candidate_owner.T,
        target.T,
    )
    parts = jnp.sum(send_all(parts, "cand", n_cand).reshape(n_cand, own, -1), 0)
    total = parts[:, 2 * hidden : 2 * hidden + 1]
    losses = jnp.log(total[:, 0]) - parts[:, 2 * hidden + 1]
    d_user = parts[:, :hidden] / (0.25 * total) - parts[:, hidden : 2 * hidden]
    d_user = d_user * score_weights
    d_picked = mm_split(d_user, user_full, ((1,), (1,)))
    d_gated = mm_split(d_picked, merge_weights, ((1,), (1,)))
    d_attended = norm_back(d_gated * gate, normed, inverse).astype(BF16)
    d_before_gate = (d_gated * normed * slope_request[:own, :HEAD]).astype(BF16)

    blocks = features // HEAD

    def strips_of(wide):
        wide = wide.reshape(own, blocks, HEAD).transpose(1, 0, 2)
        return jnp.repeat(wide, n_ctx // blocks, axis=0)

    shared = jnp.concatenate([d_attended, gated, d_before_gate], 0)
    sent = jnp.concatenate(
        [
            jnp.broadcast_to(shared[None], (n_ctx,) + shared.shape),
            strips_of(d_picked.astype(BF16)),
        ],
        1,
    )
    sent = swap(sent, "ctx")
    all_grads = sent[:, :own].reshape(requests, HEAD)
    all_gated = sent[:, own : 2 * own].reshape(requests, HEAD)
    all_gate_grads = sent[:, 2 * own : 3 * own].reshape(requests, HEAD)
    d_block = sent[:, 3 * own :].reshape(requests, HEAD)
    lane = lax.rem(ctx, n_ctx // blocks) * strip
    grad_merge = mm(d_block, all_gated, ((0,), (0,)))
    grad_merge = lax.dynamic_slice_in_dim(grad_merge, lane, strip, 0).T
    slopes = mm(all_grads, values, ((1,), (1,)))
    d_logit = jnp.where(allowed, slopes * logit_slope / divisor, 0.0).astype(BF16)
    d_query = (mm(d_logit, key_heads) * scaling).astype(BF16)
    d_key = mm(d_logit, queries, ((0,), (0,))) * scaling
    d_value = mm(weight, all_grads, ((0,), (0,)))
    d_value = (d_value * slope[:, :HEAD]).astype(BF16)
    d_key = (d_key * slope[:, HEAD:]).astype(BF16)
    dense = jnp.concatenate([d_value, d_key], 1)
    dense_grad = mm(x_low, dense, ((0,), (0,))).astype(BF16)
    dense_grad = dense_grad.reshape(n_ctx, strip, 2 * HEAD)
    dense_grad = jnp.concatenate(
        [
            dense_grad[:, :, :HEAD],
            dense_grad[:, :, HEAD:],
            d_query.reshape(n_ctx, own, HEAD),
            strips_of(request_low[:own]),
        ],
        1,
    )
    dense_grad = swap(dense_grad, "ctx")
    x_block = dense_grad[:, 2 * strip + own :].reshape(requests, HEAD)
    dense_grad = jnp.sum(dense_grad[:, : 2 * strip + own].astype(F32), 0)
    own_query_grad = dense_grad[2 * strip :]
    d_before_query = (own_query_grad * slope_request[:own, HEAD:]).astype(BF16)

    back_dense = norm_back(mm(dense, weights_dense, ((1,), (1,))), x_normed, x_inverse)
    back_dense = lax.psum_scatter(
        back_dense.reshape(rows, n_cand, width).transpose(1, 0, 2).reshape(n_cand * rows, width),
        "cand",
        scatter_dimension=0,
        tiled=True,
    )
    request_before = jnp.concatenate([d_before_gate, d_before_query], 1)
    back = norm_back(
        mm(request_before, weights_request, ((1,), (1,))), r_normed[:own], r_inverse[:own]
    )
    back = back.reshape(own, n_cand, width).transpose(1, 0, 2)
    back = jnp.sum(swap(back, "cand"), 0)
    own_slice = lax.dynamic_slice_in_dim(d_picked, cand * width, width, 1)
    request_grad = back + own_slice
    final = jnp.concatenate([request_grad.astype(BF16), d_before_query], 0)
    final = send_all(final, "ctx", n_ctx)
    all_request_grad = final[:, :own].reshape(requests, width)
    all_query_grads = final[:, own:].reshape(requests, HEAD)
    history_grad = back_dense + mm(matches, all_request_grad, ((0,), (0,)))
    gate_query = mm(
        x_block, jnp.concatenate([all_gate_grads, all_query_grads], 1), ((0,), (0,))
    )
    gate_query = lax.dynamic_slice_in_dim(gate_query, lane, strip, 0)
    grad_heads = jnp.concatenate(
        [
            gate_query[:, :HEAD],
            dense_grad[:strip],
            gate_query[:, HEAD:],
            dense_grad[strip : 2 * strip],
        ],
        1,
    )
    return (losses, history_grad, grad_heads, grad_merge)


def solution(mesh):
    n_ctx = mesh.shape["ctx"]
    n_cand = mesh.shape["cand"]

    def body(*args):
        return per_device(n_ctx, n_cand, *args)

    return jax.shard_map(
        body,
        mesh=mesh,
        in_specs=(
            P("ctx", "cand"),
            P(None, "cand"),
            P("cand", None),
            P("cand", None),
            P("cand", None),
            P(),
            P(),
            P(),
            P("ctx", None),
            P("ctx", None),
            P("ctx", None),
        ),
        out_specs=(P("ctx"), P("ctx", "cand"), P("ctx", "cand"), P("cand", "ctx")),
        check_vma=False,
    )
```
